32 devices in a mesh: dom: 8 (over z, y), group: 4 (over x, core).
Axes of the slice: x: 2, y: 2, z: 4, core: 2. Of those that a mesh axis runs over, the one named last changes fastest.
Arguments:
- embeddings: float32 [8192, 400], P(('dom', 'group')), may hold values from -3 to 3
- adagrad_state: float32 [8192], P(('dom', 'group')), may hold values from 0.05 to 0.5
- relation_diag: float32 [64, 400], replicated, may hold values from 0.1 to 1.9
- bucket_counts: int32 [2, 8], P(None, 'dom'), may hold values from 512 to 4096, as said below
- src_index: int32 [2, 8, 4096], P(None, 'dom', 'group'), may hold values from 0 to 1023
- dst_index: int32 [2, 8, 4096], P(None, 'dom', 'group'), may hold values from 0 to 1023
- rel_index: int32 [2, 8, 4096], P(None, 'dom', 'group'), may hold values from 0 to 63
- neg_index: int32 [2, 8, 4, 1024], P(None, 'dom', 'group'), may hold values from 0 to 1023
Outputs:
- new_embeddings: float32 [8192, 400], P(('dom', 'group'))
- new_state: float32 [8192], P(('dom', 'group'))
The draws below stay inside these ranges and needn't reach their ends.
Inputs may be any that keep to these rules, and one draw needn't show every extreme that they name: bucket_counts holds the live edges of each bucket; live slots are the first ones of the bucket; at least one bucket is full and at least one holds exactly 512 live edges.
All inputs are finite; a program needn't handle non-finite values.
Results may differ from the reference program's by a relative error of at most 0.0016.
Values may be sent and summed in bfloat16 or wider, within the bound.
A program may use at most 64 MiB of HBM per device.

```python
import math
from functools import partial
import jax
import jax.numpy as jnp
from jax import lax

D = 400
EDGE_DEV = 1024
NEG = 1024
ROUNDS = 2
RELS = 64
PART = 1024
EDGES = 4096
ENT = 8192
N_DOM = 8
N_GROUP = 4


def draw_bucket_counts(key, part):
    key_base, key_pick = jax.random.split(key, 2)
    counts = jax.random.randint(key_base, (ROUNDS, N_DOM), EDGES // 8, EDGES + 1)
    flat_counts = counts.reshape(-1)
    picked = jax.random.permutation(key_pick, ROUNDS * N_DOM)
    flat_counts = flat_counts.at[picked[0]].set(EDGES).at[picked[1]].set(EDGES // 8)
    return flat_counts.reshape(ROUNDS, N_DOM).astype(jnp.int32)


def with_ends(result, stream_key, low, top_value):
    longest = result.shape.index(max(result.shape))
    spots = []
    for shift in (0, 1):
        where = [jax.random.randint(jax.random.fold_in(stream_key, axis), (), 0, length) for axis, length in enumerate(result.shape)]
        where[longest] = (where[longest] + shift) % result.shape[longest]
        spots.append(tuple(where))
    return result.at[spots[0]].set(low).at[spots[1]].set(top_value)


def shard_levels(key, dims, pieces, smallest, high):
    def one(position, blocks):
        steps = jax.random.uniform(jax.random.fold_in(jax.random.fold_in(key, 6), position), (blocks,), jnp.float32, smallest / len(pieces), high / len(pieces))
        return jnp.repeat(jnp.exp(steps), dims[position] // blocks).reshape((-1,) + (1,) * (len(dims) - position - 1))

    factor_of = one(*pieces[0])
    for cut in pieces[1:]:
        factor_of = factor_of * one(*cut)
    return factor_of


def centred(stream_key, shape, spread, limit, cuts=(), kind=jnp.bfloat16):
    drawn = jax.random.normal(stream_key, shape, jnp.float32) * spread
    if len(cuts) > 0:
        drawn = shard_levels(stream_key, shape, cuts, -0.22, 0.18) * drawn
    return jnp.clip(drawn, min=-limit, max=limit).astype(kind)


def setup_inputs(seed: int = 0) -> dict:
    streams_of = jax.random.split(jax.random.key(seed), 9)
    return {
        "embeddings": centred(streams_of[0], (ENT, D), 0.5, 3.0, ((0, 32),), jnp.float32),
        "adagrad_state": jnp.clip(jnp.exp(math.log(0.5) - 2.3025851 * jax.random.uniform(streams_of[1], (ENT,), jnp.float32) ** shard_levels(streams_of[1], (ENT,), ((0, 32),), -0.2, 0.2)), 0.05, 0.5),
        "relation_diag": jnp.clip(1.0 + 0.18 * jax.random.normal(streams_of[2], (RELS, D), jnp.float32), 0.1, 1.9),
        "bucket_counts": draw_bucket_counts(jax.random.fold_in(streams_of[8], 71), 0),
        "src_index": with_ends(jax.random.randint(streams_of[4], (ROUNDS, N_DOM, EDGES), 0, PART), jax.random.fold_in(streams_of[4], 1), 0, PART - 1).astype(jnp.int32),
        "dst_index": with_ends(jax.random.randint(streams_of[5], (ROUNDS, N_DOM, EDGES), 0, PART), jax.random.fold_in(streams_of[5], 1), 0, PART - 1).astype(jnp.int32),
        "rel_index": with_ends(jax.random.randint(streams_of[6], (ROUNDS, N_DOM, EDGES), 0, RELS), jax.random.fold_in(streams_of[6], 1), 0, RELS - 1).astype(jnp.int32),
        "neg_index": with_ends(jax.random.randint(streams_of[7], (ROUNDS, N_DOM, N_GROUP, NEG), 0, PART), jax.random.fold_in(streams_of[7], 1), 0, PART - 1).astype(jnp.int32),
    }


LEARN_RATE = 0.1
ROW_EPS = 1e-06

def block_terms(lhs_block, rhs_block, relation_diag, src_ids, dst_ids, rel_ids, neg_ids, live_mask):
    lhs_rows = jnp.take(lhs_block, src_ids, axis=0).astype(jnp.float32)
    rhs_rows = jnp.take(rhs_block, dst_ids, axis=0).astype(jnp.float32)
    neg_rows = jnp.take(rhs_block, neg_ids, axis=0).astype(jnp.float32)
    rel_rows = jnp.take(relation_diag, rel_ids, axis=0)
    query_rows = lhs_rows * rel_rows
    query_half = lax.optimization_barrier(query_rows.astype(jnp.bfloat16)).astype(jnp.float32)
    pos_score = lax.optimization_barrier(jnp.sum(query_rows * rhs_rows, axis=1))
    scores = jnp.dot(query_half, neg_rows.T, precision=lax.Precision.HIGHEST)
    weights = (live_mask[:, None] * jax.nn.sigmoid(scores) / NEG).astype(jnp.bfloat16)
    weights = lax.optimization_barrier(weights).astype(jnp.float32)
    pos_coef = -live_mask * jax.nn.sigmoid(-pos_score)
    grad_query = pos_coef[:, None] * rhs_rows + jnp.dot(weights, neg_rows, precision=lax.Precision.HIGHEST)
    grad_neg = jnp.dot(weights.T, query_half, precision=lax.Precision.HIGHEST)
    return (grad_query * rel_rows, pos_coef[:, None] * query_rows, grad_neg)

def reference(embeddings, adagrad_state, relation_diag, bucket_counts, src_index, dst_index, rel_index, neg_index):
    emb_half = embeddings.astype(jnp.bfloat16)
    blocks = emb_half.reshape(N_DOM, PART, D)
    slot_ids = jnp.arange(EDGES, dtype=jnp.int32).reshape(N_GROUP, EDGE_DEV)

    def worker(loop_index, grad_table):
        worker_id = jnp.asarray(loop_index).astype(jnp.int32)
        lhs_block = lax.dynamic_index_in_dim(blocks, worker_id, 0, keepdims=False)
        for turn_index in range(ROUNDS):
            far_part = jnp.mod(worker_id - (turn_index + 1), N_DOM).astype(jnp.int32)
            rhs_block = lax.dynamic_index_in_dim(blocks, far_part, 0, keepdims=False)
            live_count = lax.dynamic_index_in_dim(bucket_counts[turn_index], worker_id, 0, keepdims=False)
            live_mask = (slot_ids < live_count).astype(jnp.float32)
            src_ids = lax.dynamic_index_in_dim(src_index[turn_index], worker_id, 0, keepdims=False).reshape(N_GROUP, EDGE_DEV)
            dst_ids = lax.dynamic_index_in_dim(dst_index[turn_index], worker_id, 0, keepdims=False).reshape(N_GROUP, EDGE_DEV)
            rel_ids = lax.dynamic_index_in_dim(rel_index[turn_index], worker_id, 0, keepdims=False).reshape(N_GROUP, EDGE_DEV)
            neg_ids = lax.dynamic_index_in_dim(neg_index[turn_index], worker_id, 0, keepdims=False)
            terms = jax.vmap(partial(block_terms, lhs_block, rhs_block, relation_diag))(src_ids, dst_ids, rel_ids, neg_ids, live_mask)
            lhs_sum = jax.ops.segment_sum(terms[0].reshape(-1, D), src_ids.reshape(-1), PART)
            rhs_sum = jax.ops.segment_sum(terms[1].reshape(-1, D), dst_ids.reshape(-1), PART)
            rhs_sum = rhs_sum + jax.ops.segment_sum(terms[2].reshape(-1, D), neg_ids.reshape(-1), PART)
            grad_table = grad_table.at[worker_id].add(lhs_sum)
            grad_table = grad_table.at[far_part].add(rhs_sum)
        return grad_table
    grad_table = lax.fori_loop(0, N_DOM, worker, jnp.zeros((N_DOM, PART, D), jnp.float32))
    grad_total = grad_table.reshape(ENT, D)
    new_state = adagrad_state + lax.optimization_barrier(jnp.mean(grad_total * grad_total, axis=1))
    new_embeddings = embeddings - LEARN_RATE * grad_total / (jnp.sqrt(new_state)[:, None] + ROW_EPS)
    return (new_embeddings, new_state)
```

```python
import jax
import jax.numpy as jnp
from jax import lax
from jax.experimental import pallas as pl
from jax.experimental.pallas import tpu as pltpu
from jax.sharding import PartitionSpec as P

ROUNDS = 2
LEARN_RATE = 0.1
ROW_EPS = 1e-06
MESH = pl.DeviceIdType.MESH
BF = jnp.bfloat16
F32 = jnp.float32


def dot_nn(a, b):
    return lax.dot_general(a, b, (((1,), (0,)), ((), ())), preferred_element_type=F32)


def dot_nt(a, b):
    return lax.dot_general(a, b, (((1,), (1,)), ((), ())), preferred_element_type=F32)


def dot_tn(a, b):
    return lax.dot_general(a, b, (((0,), (0,)), ((), ())), preferred_element_type=F32)


def logistic(x):
    return 0.5 * jnp.tanh(0.5 * x) + 0.5


def kernel(
    n_dom,
    n_group,
    neg_slots,
    counts_ref,
    emb_ref,
    state_ref,
    rel_ref,
    src_ref,
    dst_ref,
    relid_ref,
    neg_ref,
    out_ref,
    new_state_ref,
    parts,
    src_hot,
    query,
    query_half,
    rel_rows,
    grad_query,
    lhs_sum,
    outbox,
    core_in,
    pair_out,
    pair_in,
    far_out,
    far_in,
    send_sem,
    recv_sem,
):
    w = lax.axis_index("dom")
    g = lax.axis_index("group")
    width, quarter = emb_ref.shape
    edges = src_ref.shape[2]
    core = lax.rem(g, 2)
    core_g = g + 1 - 2 * core
    half_g = lax.rem(g + 2, n_group)
    both_g = lax.rem(core_g + 2, n_group)

    def to(dom, group):
        return (dom, group)

    def dom_at(distance):
        return lax.rem(w + n_dom + distance, n_dom)

    barrier = pltpu.get_barrier_semaphore()
    friends = [(w, core_g), (w, half_g)]
    for k in range(1, ROUNDS + 1):
        friends += [(dom_at(k), g), (dom_at(-k), g)]
    for friend in friends:
        pl.semaphore_signal(barrier, inc=1, device_id=friend, device_id_type=MESH)

    parts[0, g] = emb_ref[...].astype(BF)
    pl.semaphore_wait(barrier, len(friends))

    used = [0]

    def send(src, dst, device):
        i = used[0]
        used[0] += 1
        copy = pltpu.make_async_remote_copy(
            src_ref=src,
            dst_ref=dst,
            send_sem=send_sem.at[i],
            recv_sem=recv_sem.at[i],
            device_id=device,
            device_id_type=MESH,
        )
        copy.start()
        return copy

    pending = []

    def spread(k):
        a = send(parts.at[k, g], parts.at[k, g], (w, half_g))
        b = send(parts.at[k, g], parts.at[k, g], (w, core_g))
        return a, b

    def forward(k, copies):
        copies[0].wait_recv()
        c = send(parts.at[k, half_g], parts.at[k, half_g], (w, core_g))
        pending.extend([copies[0], copies[1], c])
        return copies[1], c

    def arrived(copies):
        for copy in copies:
            copy.wait_recv()

    far = [
        send(parts.at[0, g], parts.at[k, g], (dom_at(k), g)) for k in range(1, ROUNDS + 1)
    ]
    pending.extend(far)
    own = spread(0)

    rel_t = rel_ref[...].T
    rel_hi = rel_t.astype(BF)
    rel_lo = (rel_t - rel_hi.astype(F32)).astype(BF)
    rel_count = rel_t.shape[1]

    def hot(ids, base, rows):
        return lax.broadcasted_iota(jnp.int32, (rows, edges), 0) + base == ids

    def hot_half(ids, base, rows):
        return jnp.where(hot(ids, base, rows), 1.0, 0.0).astype(BF)

    def queries(r):
        total = None
        src_ids = src_ref[r]
        for q in range(n_group):
            table = hot_half(src_ids, q * quarter, quarter)
            src_hot[q] = table
            part = dot_nn(parts[0, q], table)
            total = part if total is None else total + part
        rel_hot = hot_half(relid_ref[r], 0, rel_count)
        rel = dot_nn(rel_hi, rel_hot) + dot_nn(rel_lo, rel_hot)
        rel_rows[...] = rel
        value = total * rel
        query[...] = value
        query_half[...] = value.astype(BF)

    def edges_of(r):
        k = r + 1
        slot_ids = g * edges + lax.broadcasted_iota(jnp.int32, (1, edges), 1)
        live = jnp.where(slot_ids < counts_ref[r, 0], 1.0, 0.0)
        dst_ids = dst_ref[r]
        neg_ids = neg_ref[r]
        total = None
        for q in range(n_group):
            part = dot_nn(parts[k, q], hot_half(dst_ids, q * quarter, quarter))
            total = part if total is None else total + part
        pos = jnp.sum(query[...] * total, axis=0, keepdims=True)
        coef = -live * logistic(-pos)
        share = live * (1.0 / neg_slots)

        def one(q):
            block = parts[k, q]
            scores = dot_tn(block, query_half[...])
            base = q * quarter
            rows = lax.broadcasted_iota(jnp.int32, (quarter, neg_slots), 0) + base
            times = jnp.sum(jnp.where(rows == neg_ids, 1.0, 0.0), axis=1, keepdims=True)
            z = logistic(scores) * share * times
            z = (z + jnp.where(hot(dst_ids, base, quarter), coef, 0.0)).astype(BF)
            outbox[r, q] = dot_nt(query_half[...], z).astype(BF)
            return dot_nn(block, z)

        grad_query[...] = one(0)
        for q in range(1, n_group):
            grad_query[...] += one(q)

    def lhs_grads(r):
        term = (grad_query[...] * rel_rows[...]).astype(BF)
        for q in range(n_group):
            part = dot_nt(term, src_hot[q])
            if r == 0:
                lhs_sum[q] = part
            else:
                outbox[ROUNDS, q] = (lhs_sum[q] + part).astype(BF)

    def reduce_core(s):
        a = send(outbox.at[s, both_g], core_in.at[s, 0], (w, core_g))
        b = send(outbox.at[s, core_g], core_in.at[s, 1], (w, core_g))
        pending.extend([a, b])
        return a, b

    def reduce_pair(s, copies):
        copies[0].wait_recv()
        pair_out[s] = (outbox[s, half_g].astype(F32) + core_in[s, 0].astype(F32)).astype(BF)
        c = send(pair_out.at[s], pair_in.at[s], (w, half_g))
        copies[1].wait_recv()
        pending.append(c)
        return c

    def reduced(s, copy):
        mine = outbox[s, g].astype(F32) + core_in[s, 1].astype(F32)
        copy.wait_recv()
        return mine + pair_in[s].astype(F32)

    def give_back(s, copy):
        far_out[s] = reduced(s, copy).astype(BF)
        c = send(far_out.at[s], far_in.at[s], (dom_at(-(s + 1)), g))
        pending.append(c)
        return c

    own = forward(0, own)
    far[0].wait_recv()
    one = spread(1)
    arrived(own)
    far[1].wait_recv()
    two = spread(2)
    one = forward(1, one)
    queries(0)
    two = forward(2, two)
    arrived(one)
    edges_of(0)
    back = reduce_core(0)
    lhs_grads(0)
    back = reduce_pair(0, back)
    queries(1)
    back = give_back(0, back)
    arrived(two)
    edges_of(1)
    back_two = reduce_core(1)
    lhs_grads(1)
    lhs = reduce_core(ROUNDS)
    back_two = reduce_pair(1, back_two)
    lhs = reduce_pair(ROUNDS, lhs)
    back_two = give_back(1, back_two)
    grad = reduced(ROUNDS, lhs)
    back.wait_recv()
    grad = grad + far_in[0].astype(F32)
    back_two.wait_recv()
    grad = grad + far_in[1].astype(F32)
    new_state = state_ref[...] + jnp.sum(grad * grad, axis=0, keepdims=True) * (1.0 / width)
    new_state_ref[...] = new_state
    out_ref[...] = emb_ref[...] - grad * (LEARN_RATE / (jnp.sqrt(new_state) + ROW_EPS))
    for copy in pending:
        copy.wait_send()


def per_device(
    embeddings,
    adagrad_state,
    relation_diag,
    bucket_counts,
    src_index,
    dst_index,
    rel_index,
    neg_index,
):
    n_dom = lax.axis_size("dom")
    n_group = lax.axis_size("group")
    quarter, width = embeddings.shape
    edges = src_index.shape[2]
    neg_slots = neg_index.shape[3]
    copies = 2 + 3 * (ROUNDS + 1) + 4 * ROUNDS + 3
    vmem = pl.BlockSpec(memory_space=pltpu.VMEM)
    smem = pl.BlockSpec(memory_space=pltpu.SMEM)

    def body(*refs):
        kernel(n_dom, n_group, neg_slots, *refs)

    out, state = pl.pallas_call(
        body,
        out_shape=(
            jax.ShapeDtypeStruct((width, quarter), F32),
            jax.ShapeDtypeStruct((1, quarter), F32),
        ),
        in_specs=[smem] + [vmem] * 7,
        out_specs=(vmem, vmem),
        scratch_shapes=[
            pltpu.VMEM((ROUNDS + 1, n_group, width, quarter), BF),
            pltpu.VMEM((n_group, quarter, edges), BF),
            pltpu.VMEM((width, edges), F32),
            pltpu.VMEM((width, edges), BF),
            pltpu.VMEM((width, edges), F32),
            pltpu.VMEM((width, edges), F32),
            pltpu.VMEM((n_group, width, quarter), F32),
            pltpu.VMEM((ROUNDS + 1, n_group, width, quarter), BF),
            pltpu.VMEM((ROUNDS + 1, 2, width, quarter), BF),
            pltpu.VMEM((ROUNDS + 1, width, quarter), BF),
            pltpu.VMEM((ROUNDS + 1, width, quarter), BF),
            pltpu.VMEM((ROUNDS, width, quarter), BF),
            pltpu.VMEM((ROUNDS, width, quarter), BF),
            pltpu.SemaphoreType.DMA((copies,)),
            pltpu.SemaphoreType.DMA((copies,)),
        ],
        compiler_params=pltpu.CompilerParams(
            collective_id=0, has_side_effects=True, vmem_limit_bytes=52 * 1024 * 1024
        ),
    )(
        bucket_counts,
        embeddings.T,
        adagrad_state.reshape(1, quarter),
        relation_diag,
        src_index,
        dst_index,
        rel_index,
        neg_index.reshape(ROUNDS, 1, neg_slots),
    )
    return (out.T, state.reshape(quarter))


def solution(mesh):
    placed = (
        P(("dom", "group"), None),
        P(("dom", "group")),
        P(),
        P(None, "dom"),
        P(None, "dom", "group"),
        P(None, "dom", "group"),
        P(None, "dom", "group"),
        P(None, "dom", "group", None),
    )
    return jax.shard_map(
        per_device,
        mesh=mesh,
        in_specs=placed,
        out_specs=(P(("dom", "group"), None), P(("dom", "group"))),
        check_vma=False,
    )
```

```python
import jax
import jax.numpy as jnp
from jax import lax
from jax.experimental import pallas as pl
from jax.experimental.pallas import tpu as pltpu
from jax.sharding import PartitionSpec as P

ROUNDS = 2
LEARN_RATE = 0.1
ROW_EPS = 1e-06
MESH = pl.DeviceIdType.MESH
BF = jnp.bfloat16
F32 = jnp.float32


def dot_nn(a, b):
    return lax.dot_general(a, b, (((1,), (0,)), ((), ())), preferred_element_type=F32)


def dot_nt(a, b):
    return lax.dot_general(a, b, (((1,), (1,)), ((), ())), preferred_element_type=F32)


def dot_tn(a, b):
    return lax.dot_general(a, b, (((0,), (0,)), ((), ())), preferred_element_type=F32)


def logistic(x):
    return 0.5 * jnp.tanh(0.5 * x) + 0.5


def kernel(
    n_dom,
    n_group,
    neg_slots,
    counts_ref,
    emb_hbm,
    state_hbm,
    rel_hbm,
    src_hbm,
    dst_hbm,
    relid_hbm,
    neg_hbm,
    out_ref,
    new_state_ref,
    emb_ref,
    state_ref,
    rel_ref,
    src_ref,
    dst_ref,
    relid_ref,
    neg_ref,
    parts,
    src_hot,
    dst_hot,
    times_of,
    query,
    query_half,
    rel_rows,
    grad_query,
    lhs_sum,
    outbox,
    core_in,
    pair_out,
    pair_in,
    far_out,
    far_in,
    load_sem,
    send_sem,
    recv_sem,
):
    w = lax.axis_index("dom")
    g = lax.axis_index("group")
    width, quarter = emb_ref.shape
    edges = src_ref.shape[2]
    core = lax.rem(g, 2)
    core_g = g + 1 - 2 * core
    half_g = lax.rem(g + 2, n_group)
    both_g = lax.rem(core_g + 2, n_group)

    def to(dom, group):
        return (dom, group)

    def dom_at(distance):
        return lax.rem(w + n_dom + distance, n_dom)

    barrier = pltpu.get_barrier_semaphore()
    friends = [(w, core_g), (w, half_g)]
    for k in range(1, ROUNDS + 1):
        friends += [(dom_at(k), g), (dom_at(-k), g)]
    for friend in friends:
        pl.semaphore_signal(barrier, inc=1, device_id=friend, device_id_type=MESH)

    fetches = []
    far_refs = (emb_hbm, rel_hbm, src_hbm, relid_hbm, neg_hbm, dst_hbm, state_hbm)
    near_refs = (emb_ref, rel_ref, src_ref, relid_ref, neg_ref, dst_ref, state_ref)
    for i, (src, dst) in enumerate(zip(far_refs, near_refs)):
        fetch = pltpu.make_async_copy(src, dst, load_sem.at[i])
        fetch.start()
        fetches.append(fetch)
    fetches[0].wait()
    parts[0, g] = emb_ref[...].astype(BF)
    pl.semaphore_wait(barrier, len(friends))

    used = [0]

    def send(src, dst, device):
        i = used[0]
        used[0] += 1
        copy = pltpu.make_async_remote_copy(
            src_ref=src,
            dst_ref=dst,
            send_sem=send_sem.at[i],
            recv_sem=recv_sem.at[i],
            device_id=device,
            device_id_type=MESH,
        )
        copy.start()
        return copy

    pending = []

    def spread(k):
        a = send(parts.at[k, g], parts.at[k, g], (w, half_g))
        b = send(parts.at[k, g], parts.at[k, g], (w, core_g))
        return a, b

    def forward(k, copies):
        copies[0].wait_recv()
        c = send(parts.at[k, half_g], parts.at[k, half_g], (w, core_g))
        pending.extend([copies[0], copies[1], c])
        return copies[1], c

    def arrived(copies):
        for copy in copies:
            copy.wait_recv()

    own = spread(0)
    far = [
        send(parts.at[0, g], parts.at[k, g], (dom_at(k), g)) for k in range(1, ROUNDS + 1)
    ]
    pending.extend(far)
    for fetch in fetches[1:]:
        fetch.wait()

    rel_t = rel_ref[...].T
    rel_hi = rel_t.astype(BF)
    rel_lo = (rel_t - rel_hi.astype(F32)).astype(BF)
    rel_count = rel_t.shape[1]
    order = (both_g, core_g, half_g, g)

    def hot(ids, base, rows):
        return lax.broadcasted_iota(jnp.int32, (rows, edges), 0) + base == ids

    def hot_half(ids, base, rows):
        return jnp.where(hot(ids, base, rows), 1.0, 0.0).astype(BF)

    def tables(r):
        for q in range(n_group):
            src_hot[r, q] = hot_half(src_ref[r], q * quarter, quarter)
            dst_hot[r, q] = hot_half(dst_ref[r], q * quarter, quarter)
            named = lax.broadcasted_iota(jnp.int32, (quarter, neg_slots), 0) + q * quarter
            named = jnp.where(named == neg_ref[r], 1.0, 0.0)
            times_of[r, q] = jnp.sum(named, axis=1, keepdims=True)
        rel_hot = hot_half(relid_ref[r], 0, rel_count)
        rel_rows[r] = dot_nn(rel_hi, rel_hot) + dot_nn(rel_lo, rel_hot)

    def gathered(k, table):
        total = None
        for q in range(n_group):
            part = dot_nn(parts[k, q], table[q])
            total = part if total is None else total + part
        return total

    def queries(r):
        value = gathered(0, src_hot.at[r]) * rel_rows[r]
        query[r] = value
        query_half[r] = value.astype(BF)

    def live_of(r):
        slot_ids = g * edges + lax.broadcasted_iota(jnp.int32, (1, edges), 1)
        return jnp.where(slot_ids < counts_ref[0, r], 1.0, 0.0)

    def coef_of(r):
        pos = jnp.sum(query[r] * gathered(r + 1, dst_hot.at[r]), axis=0, keepdims=True)
        return -live_of(r) * logistic(-pos)

    def edges_of(r, coef):
        share = live_of(r) * (1.0 / neg_slots)
        copies = []
        for i, q in enumerate(order):
            block = parts[r + 1, q]
            scores = dot_tn(block, query_half[r])
            z = logistic(scores) * share * times_of[r, q]
            z = (z + dst_hot[r, q].astype(F32) * coef).astype(BF)
            outbox[r, q] = dot_nt(query_half[r], z).astype(BF)
            if i < 2:
                copies.append(send(outbox.at[r, q], core_in.at[r, i], (w, core_g)))
            part = dot_nn(block, z)
            if i == 0:
                grad_query[...] = part
            else:
                grad_query[...] += part
        pending.extend(copies)
        return copies

    def lhs_grads(r):
        term = (grad_query[...] * rel_rows[r]).astype(BF)
        copies = []
        for i, q in enumerate(order):
            part = dot_nt(term, src_hot[r, q])
            if r == 0:
                lhs_sum[q] = part
                continue
            outbox[ROUNDS, q] = (lhs_sum[q] + part).astype(BF)
            if i < 2:
                copies.append(send(outbox.at[ROUNDS, q], core_in.at[ROUNDS, i], (w, core_g)))
        pending.extend(copies)
        return copies

    def reduce_pair(s, copies):
        copies[0].wait_recv()
        pair_out[s] = (outbox[s, half_g].astype(F32) + core_in[s, 0].astype(F32)).astype(BF)
        c = send(pair_out.at[s], pair_in.at[s], (w, half_g))
        copies[1].wait_recv()
        pending.append(c)
        return c

    def reduced(s, copy):
        mine = outbox[s, g].astype(F32) + core_in[s, 1].astype(F32)
        copy.wait_recv()
        return mine + pair_in[s].astype(F32)

    def give_back(s, copy):
        far_out[s] = reduced(s, copy).astype(BF)
        c = send(far_out.at[s], far_in.at[s], (dom_at(-(s + 1)), g))
        pending.append(c)
        return c

    far[0].wait_recv()
    one = spread(1)
    tables(0)
    own = forward(0, own)
    far[1].wait_recv()
    two = spread(2)
    tables(1)
    arrived(own)
    queries(0)
    one = forward(1, one)
    queries(1)
    arrived(one)
    coef = coef_of(0)
    two = forward(2, two)
    back = edges_of(0, coef)
    back = reduce_pair(0, back)
    lhs_grads(0)
    arrived(two)
    coef = coef_of(1)
    back = give_back(0, back)
    back_two = edges_of(1, coef)
    back_two = reduce_pair(1, back_two)
    lhs = lhs_grads(1)
    lhs = reduce_pair(ROUNDS, lhs)
    back_two = give_back(1, back_two)
    grad = reduced(ROUNDS, lhs)
    back.wait_recv()
    grad = grad + far_in[0].astype(F32)
    back_two.wait_recv()
    grad = grad + far_in[1].astype(F32)
    new_state = state_ref[...] + jnp.sum(grad * grad, axis=0, keepdims=True) * (1.0 / width)
    new_state_ref[...] = new_state
    out_ref[...] = emb_ref[...] - grad * (LEARN_RATE / (jnp.sqrt(new_state) + ROW_EPS))
    for copy in pending:
        copy.wait_send()


def per_device(
    embeddings,
    adagrad_state,
    relation_diag,
    bucket_counts,
    src_index,
    dst_index,
    rel_index,
    neg_index,
):
    n_dom = lax.axis_size("dom")
    n_group = lax.axis_size("group")
    quarter, width = embeddings.shape
    edges = src_index.shape[2]
    neg_slots = neg_index.shape[3]
    copies = 2 + 3 * (ROUNDS + 1) + 4 * ROUNDS + 3
    vmem = pl.BlockSpec(memory_space=pltpu.VMEM)
    smem = pl.BlockSpec(memory_space=pltpu.SMEM)

    def body(*refs):
        kernel(n_dom, n_group, neg_slots, *refs)

    out, state = pl.pallas_call(
        body,
        out_shape=(
            jax.ShapeDtypeStruct((width, quarter), F32),
            jax.ShapeDtypeStruct((1, quarter), F32),
        ),
        in_specs=[smem] + [pl.BlockSpec(memory_space=pl.ANY)] * 7,
        out_specs=(vmem, vmem),
        scratch_shapes=[
            pltpu.VMEM((width, quarter), F32),
            pltpu.VMEM((1, quarter), F32),
            pltpu.VMEM(relation_diag.shape, F32),
            pltpu.VMEM((ROUNDS, 1, edges), jnp.int32),
            pltpu.VMEM((ROUNDS, 1, edges), jnp.int32),
            pltpu.VMEM((ROUNDS, 1, edges), jnp.int32),
            pltpu.VMEM((ROUNDS, 1, neg_slots), jnp.int32),
            pltpu.VMEM((ROUNDS + 1, n_group, width, quarter), BF),
            pltpu.VMEM((ROUNDS, n_group, quarter, edges), BF),
            pltpu.VMEM((ROUNDS, n_group, quarter, edges), BF),
            pltpu.VMEM((ROUNDS, n_group, quarter, 1), F32),
            pltpu.VMEM((ROUNDS, width, edges), F32),
            pltpu.VMEM((ROUNDS, width, edges), BF),
            pltpu.VMEM((ROUNDS, width, edges), F32),
            pltpu.VMEM((width, edges), F32),
            pltpu.VMEM((n_group, width, quarter), F32),
            pltpu.VMEM((ROUNDS + 1, n_group, width, quarter), BF),
            pltpu.VMEM((ROUNDS + 1, 2, width, quarter), BF),
            pltpu.VMEM((ROUNDS + 1, width, quarter), BF),
            pltpu.VMEM((ROUNDS + 1, width, quarter), BF),
            pltpu.VMEM((ROUNDS, width, quarter), BF),
            pltpu.VMEM((ROUNDS, width, quarter), BF),
            pltpu.SemaphoreType.DMA((7,)),
            pltpu.SemaphoreType.DMA((copies,)),
            pltpu.SemaphoreType.DMA((copies,)),
        ],
        compiler_params=pltpu.CompilerParams(
            collective_id=0, has_side_effects=True, vmem_limit_bytes=52 * 1024 * 1024
        ),
    )(
        bucket_counts.T,
        embeddings.T,
        adagrad_state.reshape(1, quarter),
        relation_diag,
        src_index,
        dst_index,
        rel_index,
        neg_index.reshape(ROUNDS, 1, neg_slots),
    )
    return (out.T, state.reshape(quarter))


def solution(mesh):
    placed = (
        P(("dom", "group"), None),
        P(("dom", "group")),
        P(),
        P(None, "dom"),
        P(None, "dom", "group"),
        P(None, "dom", "group"),
        P(None, "dom", "group"),
        P(None, "dom", "group", None),
    )
    return jax.shard_map(
        per_device,
        mesh=mesh,
        in_specs=placed,
        out_specs=(P(("dom", "group"), None), P(("dom", "group"))),
        check_vma=False,
    )
```
